512 devices in a mesh: replica: 8 (over z_hi, core), fsdp: 64 (over z_lo, y, x).
Axes of the slice: x: 4, y: 8, z: 8 (z_hi: 4, z_lo: 2; z = z_hi * 2 + z_lo), core: 2. Of those that a mesh axis runs over, the one named last changes fastest.
Arguments:
- activations: bfloat16 [8, 8192, 4096], P('replica', 'fsdp'), may hold values from -6 to 6
- weight: bfloat16 [8, 4096, 512], P('replica', 'fsdp'), may hold values from -0.09375 to 0.09375
- cotangent: bfloat16 [8, 8192, 512], P('replica', 'fsdp'), may hold values from -6 to 6
- quantized: int32 [8, 1048576], P('replica', 'fsdp'), may hold values from -127 to 127
- scales: float32 [8, 4096], P('replica', 'fsdp'), may hold values from 0.004 to 0.04
- outer_params: float32 [1048576], P('fsdp'), may hold values from -6 to 6
- momentum: float32 [1048576], P('fsdp'), may hold values from -6 to 6
Outputs:
- projected: bfloat16 [8, 8192, 512], P('replica', 'fsdp')
- input_grad: bfloat16 [8, 8192, 4096], P('replica', 'fsdp')
- weight_grad: bfloat16 [8, 4096, 512], P('replica', 'fsdp')
- new_params: float32 [1048576], P('fsdp')
- new_momentum: float32 [1048576], P('fsdp')
The draws below stay inside these ranges and needn't reach their ends.
Inputs may be any that keep to these rules, and one draw needn't show every extreme that they name: `quantized`: signed 8-bit codes.
All inputs are finite; a program needn't handle non-finite values.
Results may differ from the reference program's by a relative error of at most 0.008.
Values may be sent and summed in bfloat16 or wider, within the bound.
A program may use at most 64 MiB of HBM per device.

```python
import math
import jax
import jax.numpy as jnp
from jax import lax

D = 4096
KV = 512
BLOCK = 256
TOKENS = 8192
FRAG = 1048576
NBLK = 4096
N_REPLICA = 8


def with_ends(values, rng, smallest, top_value):
    extent = values.shape
    place = [jax.random.randint(jax.random.fold_in(rng, axis), (), 0, extent[axis]) for axis in range(len(extent))]
    values = values.at[tuple(place)].set(smallest)
    longest = extent.index(max(extent))
    place[longest] = (place[longest] + 1) % extent[longest]
    return values.at[tuple(place)].set(top_value)


def block_scale(own_key, shape, split, low, largest):
    gain = 1.0
    for position, blocks in split:
        heights = jax.random.uniform(jax.random.fold_in(jax.random.fold_in(own_key, 6), position), (blocks,), jnp.float32, low / len(split), largest / len(split))
        gain = gain * jnp.repeat(jnp.exp(heights), shape[position] // blocks).reshape((-1,) + (1,) * (len(shape) - 1 - position))
    return gain


def gaussian(own_key, extent, width, limit, split=(), kind=jnp.bfloat16):
    loudness = block_scale(own_key, extent, split, -0.22, 0.18) if split else 1.0
    entries = jax.random.normal(own_key, extent, jnp.float32) * width * loudness
    return jnp.minimum(jnp.maximum(entries, -limit), limit).astype(kind)


def setup_inputs(seed: int = 0) -> dict:
    streams_of = jax.random.split(jax.random.key(seed), 8)
    activations = gaussian(streams_of[0], (N_REPLICA, TOKENS, D), 1.0, 6.0, ((0, 8), (1, 64)))
    weight = gaussian(streams_of[1], (N_REPLICA, D, KV), D ** -0.5, 0.09375, ((0, 8), (1, 64)))
    cotangent = gaussian(streams_of[2], (N_REPLICA, TOKENS, KV), 1.0, 6.0, ((0, 8), (1, 64)))
    quantized = with_ends(jax.random.randint(streams_of[3], (N_REPLICA, FRAG), -127, 128), jax.random.fold_in(streams_of[3], 1), -127, 127).astype(jnp.int32)
    scales = jnp.clip(jnp.exp(math.log(0.04) - 2.30258502 * jax.random.uniform(streams_of[4], (N_REPLICA, NBLK), jnp.float32) ** block_scale(streams_of[4], (N_REPLICA, NBLK), ((0, 8), (1, 64)), -0.2, 0.2)), 0.004, 0.04)
    outer_params = gaussian(streams_of[5], (FRAG,), 1.0, 6.0, ((0, 64),), jnp.float32)
    momentum = gaussian(streams_of[6], (FRAG,), 1.0, 6.0, ((0, 64),), jnp.float32)
    return dict(activations=activations, weight=weight, cotangent=cotangent, quantized=quantized, scales=scales, outer_params=outer_params, momentum=momentum)


def one_replica(operands):
    rows, matrix, grads = operands
    output = jnp.dot(rows, matrix, preferred_element_type=jnp.float32).astype(jnp.bfloat16)
    back = lax.dot_general(grads, matrix, (((1,), (1,)), ((), ())), preferred_element_type=jnp.float32).astype(jnp.bfloat16)
    gradient = lax.dot_general(rows, grads, (((0,), (0,)), ((), ())), preferred_element_type=jnp.float32).astype(jnp.bfloat16)
    return output, back, gradient


def reference(activations, weight, cotangent, quantized, scales, outer_params, momentum):
    projected, input_grad, weight_grad = lax.map(one_replica, (activations, weight, cotangent))
    dequant = quantized.astype(jnp.float32).reshape(N_REPLICA, NBLK, BLOCK) * scales[:, :, None]
    delta = jnp.sum(dequant, axis=0).reshape(FRAG) / N_REPLICA
    new_momentum = 0.9 * momentum + delta
    new_params = outer_params - 0.7 * (delta + 0.9 * new_momentum)
    return projected, input_grad, weight_grad, new_params, new_momentum
```

```python
import functools

import jax
import jax.numpy as jnp
from jax import lax
from jax.experimental import pallas as pl
from jax.experimental.pallas import tpu as pltpu
from jax.sharding import PartitionSpec as P

X, Y, Z, R = 4, 8, 2, 8
TOK, D, KV, SHARD = 128, 4096, 512, 64
HALF = D // Z
BLK = HALF // Y
HROWS = SHARD // 2
QROWS = HROWS // 2
SIDE = 128
PIECE = SIDE // R
MAXSEM = 256
ORDER = (4, 3, -3, 2, -2, 1, -1, 0)
BF, F32 = jnp.bfloat16, jnp.float32


def kernel(
    act, wsh, cot, quant, scale, par_in, mom_in,
    proj_out, ig_out, wg_out, par_out, mom_out,
    abuf, cbuf, wbuf, g0, g1, r0, x1, s1, r1, x0, da_own, da_far,
    p_send, p_recv, p_stage, wg_stage, term, r_rep, delta, qv, sv, pv, mv, pacc,
    send, recv, local,
):
    rep = lax.axis_index("replica")
    me = lax.axis_index("fsdp")
    z = lax.div(me, X * Y)
    y = lax.rem(lax.div(me, X), Y)
    x = lax.rem(me, X)
    far = 1 - z

    def at(zz, yy, xx):
        return (rep, zz * (X * Y) + yy * X + xx)

    def yk(k):
        return lax.rem(y + (k + Y), Y)

    def xk(j):
        return lax.rem(x + (j + X), X)

    z_dev = at(far, y, x)
    y_dev = {1: at(z, yk(1), x), -1: at(z, yk(-1), x)}
    x_dev = {j: at(z, y, xk(j)) for j in (1, 2, 3)}

    def r_dev(i):
        return (lax.rem(rep + i, R), me)

    ids = {}
    started = []

    def sem(key):
        return ids.setdefault(key, len(ids))

    def push(key, src, dst, dev):
        i = sem(key)
        copy = pltpu.make_async_remote_copy(
            src_ref=src, dst_ref=dst, send_sem=send.at[i], recv_sem=recv.at[i],
            device_id=dev, device_id_type=pl.DeviceIdType.MESH)
        copy.start()
        started.append(copy)

    def arrive(key, dst):
        i = sem(key)
        pltpu.make_async_remote_copy(
            src_ref=dst, dst_ref=dst, send_sem=send.at[i], recv_sem=recv.at[i],
            device_id=z_dev, device_id_type=pl.DeviceIdType.MESH).wait_recv()

    loads = {}

    def load(key, src, dst):
        copy = pltpu.make_async_copy(src, dst, local.at[len(loads)])
        copy.start()
        loads[key] = copy

    barrier = pltpu.get_barrier_semaphore()
    peers = [z_dev, y_dev[1], y_dev[-1]] + list(x_dev.values()) + [r_dev(i) for i in range(1, R)]
    for dev in peers:
        pl.semaphore_signal(barrier, inc=1, device_id=dev, device_id_type=pl.DeviceIdType.MESH)

    def cols(zz, k):
        return pl.ds(pl.multiple_of(zz * HALF + yk(k) * BLK, BLK), BLK)

    load("q", quant, qv)
    load("s", scale, sv)
    load("w", wsh.at[0], wbuf.at[y, x])
    load("c", cot.at[0], cbuf.at[pl.ds(0, TOK)])
    for k in ORDER:
        load(("a", k), act.at[0, :, cols(z, k)], abuf.at[yk(k), pl.ds(0, TOK)])
    load("p", par_in, pv)
    load("m", mom_in, mv)

    loads["q"].wait()
    loads["s"].wait()
    owner = lax.broadcasted_iota(jnp.int32, (SIDE, SHARD), 0) // 2
    lane = lax.broadcasted_iota(jnp.int32, (SIDE, SHARD), 1)
    row_scale = jnp.sum(jnp.where(owner == lane, sv[...], 0.0), axis=1, keepdims=True)
    term[...] = (qv[...].astype(F32) * row_scale).astype(BF)

    pl.semaphore_wait(barrier, len(peers))

    rows0 = pl.ds(0, HROWS)
    rows1 = pl.ds(HROWS, HROWS)
    quarter = {1: pl.ds(HROWS, QROWS), -1: pl.ds(HROWS + QROWS, QROWS)}
    half_of = {1: 0, -1: 1}

    def pair(h):
        return pl.ds(2 * h, 2)

    def send_a(k):
        push(("a", k), act.at[0, :, cols(far, k)], abuf.at[yk(k), pl.ds(TOK, TOK)], z_dev)

    def w1_first():
        for d in (1, -1):
            push(("w1y", d, 1), wsh.at[0, rows1], wbuf.at[y, x, rows1], y_dev[d])

    def w1_to_x(k, src):
        for j in (1, 3, 2):
            push(("w1x", k, j), src, wbuf.at[yk(k), x, rows1], x_dev[j])

    def w1_step(s):
        for d in (1, -1):
            k = -d * s
            if s < 4:
                ref = wbuf.at[yk(k), x, rows1]
                arrive(("w1y", d, s), ref)
                if s < 3:
                    push(("w1y", d, s + 1), ref, ref, y_dev[d])
                else:
                    part = wbuf.at[yk(k), x, quarter[d]]
                    push(("w1y", d, 4), part, part, y_dev[d])
            else:
                arrive(("w1y", d, 4), wbuf.at[yk(4), x, quarter[d]])
        for k in ((-s, s) if s < 4 else (4,)):
            w1_to_x(k, wbuf.at[yk(k), x, rows1])

    def w0_first():
        for j in (1, 3, 2):
            push(("w0x", j), wsh.at[0, rows0], wbuf.at[y, x, rows0], x_dev[j])

    def w0_row(k, h):
        return wbuf.at[yk(k), pair(h), rows0]

    def w0_x_arrived():
        for j in (1, 3, 2):
            arrive(("w0x", j), wbuf.at[y, xk(-j), rows0])
        loads["w"].wait()
        for h in (0, 1):
            for d in (1, -1):
                push(("w0y", d, 1, h), w0_row(0, h), w0_row(0, h), y_dev[d])

    def w0_step(s):
        for h in (0, 1):
            for d in (1, -1):
                k = -d * s
                if s < 4:
                    ref = w0_row(k, h)
                    arrive(("w0y", d, s, h), ref)
                    if s < 3 or half_of[d] == h:
                        push(("w0y", d, s + 1, h), ref, ref, y_dev[d])
                elif half_of[d] == h:
                    arrive(("w0y", d, 4, h), w0_row(4, h))

    def w1_x_arrived(k):
        for j in (1, 3, 2):
            arrive(("w1x", k, j), wbuf.at[yk(k), xk(-j), rows1])

    def input_grad(k):
        w = wbuf[yk(k)].reshape(BLK, KV)
        out = lax.dot_general(cbuf[...], w, (((1,), (1,)), ((), ())),
                              preferred_element_type=F32).astype(BF)
        da_far[yk(k)] = out[TOK:]
        push(("da", k), da_far.at[yk(k)], ig_out.at[0, :, cols(z, k)], z_dev)
        da_own[yk(k)] = out[:TOK]
        load(("da", k), da_own.at[yk(k)], ig_out.at[0, :, cols(z, k)])

    def weight_grad(k):
        loads["a", k].wait()
        arrive(("a", k), abuf.at[yk(k), pl.ds(TOK, TOK)])
        g = lax.dot_general(abuf[yk(k)], cbuf[...], (((0,), (0,)), ((), ())),
                            preferred_element_type=F32).astype(BF)
        g = g.reshape(X, SHARD, KV)
        g0[yk(k)] = g[:, :HROWS]
        g1[yk(k)] = g[:, HROWS:]

    def g0_send(s, d, h, k):
        ref = g0.at[yk(k), pair(h)]
        push(("g0y", d, s, h), ref, r0.at[half_of[d], s - 1, pair(h)], y_dev[d])

    def g0_first():
        for d in (1, -1):
            g0_send(1, d, half_of[d], 4)

    def g0_step(s):
        for d in (1, -1):
            k = d * (4 - s)
            for h in (0, 1):
                if s > 1 or half_of[d] == h:
                    slot = r0.at[half_of[d], s - 1, pair(h)]
                    arrive(("g0y", d, s, h), slot)
                    own = g0.at[yk(k), pair(h)]
                    own[...] = (own[...].astype(F32) + slot[...].astype(F32)).astype(BF)
                g0_send(s + 1, d, h, k)

    def g0_end():
        for d in (1, -1):
            for h in (0, 1):
                arrive(("g0y", d, 4, h), r0.at[half_of[d], 3, pair(h)])
        g0[y] = (g0[y].astype(F32) + r0[0, 3].astype(F32) + r0[1, 3].astype(F32)).astype(BF)
        for j in (1, 3, 2):
            push(("g0x", j), g0.at[y, xk(j)], x0.at[j - 1], x_dev[j])

    def g0_final():
        total = g0[y, x].astype(F32)
        for j in (1, 3, 2):
            arrive(("g0x", j), x0.at[j - 1])
            total += x0[j - 1].astype(F32)
        wg_stage[0:HROWS] = total.astype(BF)

    def g1_to_x(k):
        for j in (1, 3, 2):
            push(("g1x", k, j), g1.at[yk(k), xk(j)], x1.at[j - 1, yk(k)], x_dev[j])

    def g1_from_x(k):
        total = g1[yk(k), x].astype(F32)
        for j in (1, 3, 2):
            arrive(("g1x", k, j), x1.at[j - 1, yk(k)])
            total += x1[j - 1, yk(k)].astype(F32)
        return total

    g_quarter = {1: pl.ds(0, QROWS), -1: pl.ds(QROWS, QROWS)}

    def g1_first():
        s1[yk(4)] = g1_from_x(4).astype(BF)
        for d in (1, -1):
            push(("g1y", d, 1), s1.at[yk(4), g_quarter[d]], r1.at[half_of[d], 0, g_quarter[d]], y_dev[d])

    def g1_step(s):
        for d in (1, -1):
            k = d * (4 - s)
            total = g1_from_x(k)
            if s == 1:
                slot = r1.at[half_of[d], 0, g_quarter[d]]
                arrive(("g1y", d, 1), slot)
                got = slot[...].astype(F32)
                parts = [total[:QROWS], total[QROWS:]]
                parts[half_of[d]] += got
                s1[yk(k), 0:QROWS] = parts[0].astype(BF)
                s1[yk(k), QROWS:HROWS] = parts[1].astype(BF)
            else:
                slot = r1.at[half_of[d], s - 1]
                arrive(("g1y", d, s), slot)
                s1[yk(k)] = (total + slot[...].astype(F32)).astype(BF)
            push(("g1y", d, s + 1), s1.at[yk(k)], r1.at[half_of[d], s], y_dev[d])

    def g1_final():
        total = g1_from_x(0)
        for d in (1, -1):
            arrive(("g1y", d, 4), r1.at[half_of[d], 3])
            total += r1[half_of[d], 3].astype(F32)
        wg_stage[HROWS:SHARD] = total.astype(BF)

    mine = pl.ds(pl.multiple_of(rep * PIECE, PIECE), PIECE)

    def rep_first():
        for i in range(1, R):
            to = lax.rem(rep + i, R)
            push(("rs", i), term.at[pl.ds(pl.multiple_of(to * PIECE, PIECE), PIECE)], r_rep.at[i - 1], r_dev(i))

    def rep_sum():
        total = term[mine, :].astype(F32)
        for i in range(1, R):
            arrive(("rs", i), r_rep.at[i - 1])
            total += r_rep[i - 1].astype(F32)
        delta[mine, :] = total.astype(BF)
        for i in range(1, R):
            push(("ag", i), delta.at[mine], delta.at[mine], r_dev(i))

    def rep_final():
        for i in range(1, R):
            src = lax.rem(rep + (R - i), R)
            arrive(("ag", i), delta.at[pl.ds(pl.multiple_of(src * PIECE, PIECE), PIECE)])
        loads["p"].wait()
        loads["m"].wait()
        step = delta[...].astype(F32) * (1.0 / R)
        moment = 0.9 * mv[...] + step
        mv[...] = moment
        pv[...] = pv[...] - 0.7 * (step + 0.9 * moment)
        load("po", pv, par_out)
        load("mo", mv, mom_out)

    def project(ks, first):
        for n, k in enumerate(ks):
            part = jnp.dot(abuf[yk(k)], wbuf[yk(k)].reshape(BLK, KV), preferred_element_type=F32)
            if first and n == 0:
                pacc[...] = part
            else:
                pacc[...] += part

    push("c", cot.at[0], cbuf.at[pl.ds(TOK, TOK)], z_dev)
    w1_first()
    w0_first()
    send_a(4)
    w1_to_x(0, wsh.at[0, rows1])
    for k in ORDER[1:]:
        send_a(k)
    rep_first()

    w1_step(1)
    w0_x_arrived()
    w1_step(2)
    loads["c"].wait()
    arrive("c", cbuf.at[pl.ds(TOK, TOK)])
    weight_grad(4)
    g0_first()
    g1_to_x(4)
    w1_step(3)
    w0_step(1)
    w1_x_arrived(0)
    input_grad(0)
    weight_grad(3)
    weight_grad(-3)
    g0_step(1)
    g1_to_x(3)
    g1_to_x(-3)
    w1_step(4)
    w0_step(2)
    for k in (-1, 1):
        w1_x_arrived(k)
        input_grad(k)
    rep_sum()
    g1_first()
    weight_grad(2)
    weight_grad(-2)
    g0_step(2)
    g1_to_x(2)
    g1_to_x(-2)
    w0_step(3)
    for k in (-2, 2):
        w1_x_arrived(k)
        input_grad(k)
    g1_step(1)
    weight_grad(1)
    weight_grad(-1)
    g0_step(3)
    g1_to_x(1)
    g1_to_x(-1)
    for k in (-3, 3):
        w1_x_arrived(k)
        input_grad(k)
    weight_grad(0)
    g1_to_x(0)
    g1_step(2)
    w0_step(4)
    w1_x_arrived(4)
    input_grad(4)
    project(ORDER, True)
    p_send[...] = pacc[TOK:].astype(BF)
    push("p", p_send, p_recv, z_dev)
    g0_end()
    g1_step(3)
    rep_final()
    g0_final()
    g1_final()
    load("wo", wg_stage, wg_out.at[0])
    arrive("p", p_recv)
    p_stage[...] = (pacc[:TOK] + p_recv[...].astype(F32)).astype(BF)
    load("pr", p_stage, proj_out.at[0])
    for k in (0, -1, 1, -2, 2, -3, 3, 4):
        arrive(("da", k), ig_out.at[0, :, cols(far, k)])
    for copy in started:
        copy.wait_send()
    for k in ORDER:
        loads["da", k].wait()
    for key in ("po", "mo", "wo", "pr"):
        loads[key].wait()


def body(activations, weight, cotangent, quantized, scales, outer_params, momentum):
    any_spec = pl.BlockSpec(memory_space=pl.ANY)
    vm = pltpu.VMEM
    out = pl.pallas_call(
        kernel,
        out_shape=(
            jax.ShapeDtypeStruct((1, TOK, KV), BF),
            jax.ShapeDtypeStruct((1, TOK, D), BF),
            jax.ShapeDtypeStruct((1, SHARD, KV), BF),
            jax.ShapeDtypeStruct((SIDE, SIDE), F32),
            jax.ShapeDtypeStruct((SIDE, SIDE), F32),
        ),
        in_specs=[any_spec] * 7,
        out_specs=[any_spec] * 5,
        scratch_shapes=[
            vm((Y, 2 * TOK, BLK), BF),
            vm((2 * TOK, KV), BF),
            vm((Y, X, SHARD, KV), BF),
            vm((Y, X, HROWS, KV), BF),
            vm((Y, X, HROWS, KV), BF),
            vm((2, 4, X, HROWS, KV), BF),
            vm((3, Y, HROWS, KV), BF),
            vm((Y, HROWS, KV), BF),
            vm((2, 4, HROWS, KV), BF),
            vm((3, HROWS, KV), BF),
            vm((Y, TOK, BLK), BF),
            vm((Y, TOK, BLK), BF),
            vm((TOK, KV), BF),
            vm((TOK, KV), BF),
            vm((TOK, KV), BF),
            vm((SHARD, KV), BF),
            vm((SIDE, SIDE), BF),
            vm((R - 1, PIECE, SIDE), BF),
            vm((SIDE, SIDE), BF),
            vm((SIDE, SIDE), jnp.int32),
            vm((1, SHARD), F32),
            vm((SIDE, SIDE), F32),
            vm((SIDE, SIDE), F32),
            vm((2 * TOK, KV), F32),
            pltpu.SemaphoreType.DMA((MAXSEM,)),
            pltpu.SemaphoreType.DMA((MAXSEM,)),
            pltpu.SemaphoreType.DMA((32,)),
        ],
        compiler_params=pltpu.CompilerParams(
            collective_id=0, has_side_effects=True, vmem_limit_bytes=40 << 20),
        cost_estimate=pl.CostEstimate(
            flops=3 * 2 * TOK * D * KV, bytes_accessed=4 << 20, transcendentals=0),
    )(
        activations, weight, cotangent, quantized.reshape(SIDE, SIDE), scales,
        outer_params.reshape(SIDE, SIDE), momentum.reshape(SIDE, SIDE),
    )
    projected, input_grad, weight_grad, new_params, new_momentum = out
    return projected, input_grad, weight_grad, new_params.reshape(-1), new_momentum.reshape(-1)


def solution(mesh):
    placed = (
        P("replica", "fsdp", None),
        P("replica", "fsdp", None),
        P("replica", "fsdp", None),
        P("replica", "fsdp"),
        P("replica", "fsdp"),
        P("fsdp"),
        P("fsdp"),
    )
    return jax.shard_map(
        body,
        mesh=mesh,
        in_specs=placed,
        out_specs=(
            P("replica", "fsdp", None),
            P("replica", "fsdp", None),
            P("replica", "fsdp", None),
            P("fsdp"),
            P("fsdp"),
        ),
        check_vma=False,
    )
```

```python
import functools

import jax
import jax.numpy as jnp
from jax import lax
from jax.experimental import pallas as pl
from jax.experimental.pallas import tpu as pltpu
from jax.sharding import PartitionSpec as P

X, Y, Z, R = 4, 8, 2, 8
TOK, D, KV, SHARD = 128, 4096, 512, 64
HALF = D // Z
BLK = HALF // Y
HROWS = SHARD // 2
QROWS = HROWS // 2
SIDE = 128
PIECE = SIDE // R
NSEND, NRECV = 14, 80
ORDER = (4, 3, -3, 2, -2, 1, -1, 0)
BF, F32 = jnp.bfloat16, jnp.float32


def kernel(
    act, wsh, cot, quant, scale, par_in, mom_in,
    proj_out, ig_out, wg_out, par_out, mom_out,
    abuf, cbuf, wbuf, g0, g1, r0, x1, s1, r1, x0, da_own, da_far,
    p_send, p_recv, p_stage, wg_stage, term, r_rep, delta, qv, sv, pv, mv, pacc,
    send, recv, local, ready,
):
    rep = lax.axis_index("replica")
    me = lax.axis_index("fsdp")
    z = lax.div(me, X * Y)
    y = lax.rem(lax.div(me, X), Y)
    x = lax.rem(me, X)
    far = 1 - z

    def at(zz, yy, xx):
        return (rep, zz * (X * Y) + yy * X + xx)

    def yk(k):
        return lax.rem(y + (k + Y), Y)

    def xk(j):
        return lax.rem(x + (j + X), X)

    z_dev = at(far, y, x)
    y_dev = {1: at(z, yk(1), x), -1: at(z, yk(-1), x)}
    x_dev = {j: at(z, y, xk(j)) for j in (1, 2, 3)}

    def r_dev(i):
        return (lax.rem(rep + i, R), me)

    send_ids, recv_ids = {}, {}

    def together(key):
        return key[:-1] if key[0] in ("w1x", "g1x", "w0x", "g0x", "rs", "ag", "da") else key

    def remote(key, src, dst, dev):
        i = send_ids.setdefault(key[0], len(send_ids))
        j = recv_ids.setdefault(together(key), len(recv_ids))
        assert i < NSEND and j < NRECV, (i, j)
        return pltpu.make_async_remote_copy(
            src_ref=src, dst_ref=dst, send_sem=send.at[i], recv_sem=recv.at[j],
            device_id=dev, device_id_type=pl.DeviceIdType.MESH)

    def push(key, src, dst, dev):
        remote(key, src, dst, dev).start()

    def arrive(key, ref):
        remote(key, ref, ref, z_dev).wait_recv()

    def sent(kind, ref):
        pltpu.make_async_remote_copy(
            src_ref=ref, dst_ref=ref, send_sem=send.at[send_ids[kind]], recv_sem=recv.at[0],
            device_id=z_dev, device_id_type=pl.DeviceIdType.MESH).wait_send()

    loads = {}

    def load(key, src, dst):
        loads[key] = pltpu.make_async_copy(src, dst, local.at[len(loads)])
        loads[key].start()

    barrier = pltpu.get_barrier_semaphore()
    peers = [z_dev, y_dev[1], y_dev[-1]] + list(x_dev.values())

    def greet(sem_ref, dev):
        pl.semaphore_signal(sem_ref, inc=1, device_id=dev, device_id_type=pl.DeviceIdType.MESH)

    for dev in peers:
        greet(barrier, dev)

    rank = rep
    late = rank >= R // 2

    def cols(zz, k):
        return pl.ds(pl.multiple_of(zz * HALF + yk(k) * BLK, BLK), BLK)

    load("q", quant, qv)
    load("s", scale, sv)
    load("w", wsh.at[0], wbuf.at[y, x])
    load("c", cot.at[0], cbuf.at[pl.ds(0, TOK)])
    for k in ORDER:
        load(("a", k), act.at[0, :, cols(z, k)], abuf.at[yk(k), pl.ds(0, TOK)])
    load("p", par_in, pv)
    load("m", mom_in, mv)

    pl.semaphore_wait(barrier, len(peers) + rank)
    for i in range(1, R):
        behind = lax.rem(rep + i, R) > rank

        @pl.when(behind)
        def _():
            greet(barrier, r_dev(i))

        @pl.when(jnp.logical_not(behind))
        def _():
            greet(ready, r_dev(i))


    rows0 = pl.ds(0, HROWS)
    rows1 = pl.ds(HROWS, HROWS)
    quarter = {1: pl.ds(HROWS, QROWS), -1: pl.ds(HROWS + QROWS, QROWS)}
    half_of = {1: 0, -1: 1}

    def pair(h):
        return pl.ds(2 * h, 2)

    def send_a(k):
        push(("a", k), act.at[0, :, cols(far, k)], abuf.at[yk(k), pl.ds(TOK, TOK)], z_dev)

    def w1_first():
        for d in (1, -1):
            push(("w1y", d, 1), wsh.at[0, rows1], wbuf.at[y, x, rows1], y_dev[d])

    def w1_to_x(k, src):
        for j in (1, 3, 2):
            push(("w1x", k, j), src, wbuf.at[yk(k), x, rows1], x_dev[j])

    def w1_step(s):
        for d in (1, -1):
            k = -d * s
            if s < 4:
                ref = wbuf.at[yk(k), x, rows1]
                arrive(("w1y", d, s), ref)
                if s < 3:
                    push(("w1y", d, s + 1), ref, ref, y_dev[d])
                else:
                    part = wbuf.at[yk(k), x, quarter[d]]
                    push(("w1y", d, 4), part, part, y_dev[d])
            else:
                arrive(("w1y", d, 4), wbuf.at[yk(4), x, quarter[d]])
        for k in ((-s, s) if s < 4 else (4,)):
            w1_to_x(k, wbuf.at[yk(k), x, rows1])

    def w0_first():
        for j in (1, 3, 2):
            push(("w0x", j), wsh.at[0, rows0], wbuf.at[y, x, rows0], x_dev[j])

    def w0_row(k, h):
        return wbuf.at[yk(k), pair(h), rows0]

    def w0_x_arrived():
        arrive(("w0x", 0), x0)
        loads["w"].wait()
        for h in (0, 1):
            for d in (1, -1):
                push(("w0y", d, 1, h), w0_row(0, h), w0_row(0, h), y_dev[d])

    def w0_step(s):
        for h in (0, 1):
            for d in (1, -1):
                k = -d * s
                if s < 4:
                    ref = w0_row(k, h)
                    arrive(("w0y", d, s, h), ref)
                    if s < 3 or half_of[d] == h:
                        push(("w0y", d, s + 1, h), ref, ref, y_dev[d])
                elif half_of[d] == h:
                    arrive(("w0y", d, 4, h), w0_row(4, h))

    def w1_x_arrived(k):
        arrive(("w1x", k, 0), x0)

    def input_grad(k):
        w = wbuf[yk(k)].reshape(BLK, KV)
        out = lax.dot_general(cbuf[...], w, (((1,), (1,)), ((), ())),
                              preferred_element_type=F32).astype(BF)
        da_far[yk(k)] = out[TOK:]
        push(("da", k), da_far.at[yk(k)], ig_out.at[0, :, cols(z, k)], z_dev)
        da_own[yk(k)] = out[:TOK]
        pltpu.make_async_copy(da_own.at[yk(k)], ig_out.at[0, :, cols(z, k)], local.at[18]).start()

    def weight_grad(k):
        loads["a", k].wait()
        arrive(("a", k), abuf.at[yk(k), pl.ds(TOK, TOK)])
        g = lax.dot_general(abuf[yk(k)], cbuf[...], (((0,), (0,)), ((), ())),
                            preferred_element_type=F32).astype(BF)
        g = g.reshape(X, SHARD, KV)
        g0[yk(k)] = g[:, :HROWS]
        g1[yk(k)] = g[:, HROWS:]

    def g0_send(s, d, h, k):
        ref = g0.at[yk(k), pair(h)]
        push(("g0y", d, s, h), ref, r0.at[half_of[d], s - 1, pair(h)], y_dev[d])

    def g0_first():
        for d in (1, -1):
            g0_send(1, d, half_of[d], 4)

    def g0_step(s):
        for d in (1, -1):
            k = d * (4 - s)
            for h in (0, 1):
                if s > 1 or half_of[d] == h:
                    slot = r0.at[half_of[d], s - 1, pair(h)]
                    arrive(("g0y", d, s, h), slot)
                    own = g0.at[yk(k), pair(h)]
                    own[...] = (own[...].astype(F32) + slot[...].astype(F32)).astype(BF)
                g0_send(s + 1, d, h, k)

    def g0_end():
        for d in (1, -1):
            for h in (0, 1):
                arrive(("g0y", d, 4, h), r0.at[half_of[d], 3, pair(h)])
        g0[y] = (g0[y].astype(F32) + r0[0, 3].astype(F32) + r0[1, 3].astype(F32)).astype(BF)
        for j in (1, 3, 2):
            push(("g0x", j), g0.at[y, xk(j)], x0.at[j - 1], x_dev[j])

    def g0_final():
        total = g0[y, x].astype(F32)
        arrive(("g0x", 0), x0)
        for j in (1, 3, 2):
            total += x0[j - 1].astype(F32)
        wg_stage[0:HROWS] = total.astype(BF)

    def g1_to_x(k):
        for j in (1, 3, 2):
            push(("g1x", k, j), g1.at[yk(k), xk(j)], x1.at[j - 1, yk(k)], x_dev[j])

    def g1_from_x(k):
        total = g1[yk(k), x].astype(F32)
        arrive(("g1x", k, 0), x0)
        for j in (1, 3, 2):
            total += x1[j - 1, yk(k)].astype(F32)
        return total

    g_quarter = {1: pl.ds(0, QROWS), -1: pl.ds(QROWS, QROWS)}

    def g1_first():
        s1[yk(4)] = g1_from_x(4).astype(BF)
        for d in (1, -1):
            push(("g1y", d, 1), s1.at[yk(4), g_quarter[d]], r1.at[half_of[d], 0, g_quarter[d]], y_dev[d])

    def g1_step(s):
        for d in (1, -1):
            k = d * (4 - s)
            total = g1_from_x(k)
            if s == 1:
                slot = r1.at[half_of[d], 0, g_quarter[d]]
                arrive(("g1y", d, 1), slot)
                got = slot[...].astype(F32)
                parts = [total[:QROWS], total[QROWS:]]
                parts[half_of[d]] += got
                s1[yk(k), 0:QROWS] = parts[0].astype(BF)
                s1[yk(k), QROWS:HROWS] = parts[1].astype(BF)
            else:
                slot = r1.at[half_of[d], s - 1]
                arrive(("g1y", d, s), slot)
                s1[yk(k)] = (total + slot[...].astype(F32)).astype(BF)
            push(("g1y", d, s + 1), s1.at[yk(k)], r1.at[half_of[d], s], y_dev[d])

    def g1_final():
        total = g1_from_x(0)
        for d in (1, -1):
            arrive(("g1y", d, 4), r1.at[half_of[d], 3])
            total += r1[half_of[d], 3].astype(F32)
        wg_stage[HROWS:SHARD] = total.astype(BF)

    mine = pl.ds(pl.multiple_of(rep * PIECE, PIECE), PIECE)

    def dequantize():
        loads["q"].wait()
        loads["s"].wait()
        owner = lax.broadcasted_iota(jnp.int32, (SIDE, SHARD), 0) // 2
        lane = lax.broadcasted_iota(jnp.int32, (SIDE, SHARD), 1)
        row_scale = jnp.sum(jnp.where(owner == lane, sv[...], 0.0), axis=1, keepdims=True)
        term[...] = (qv[...].astype(F32) * row_scale).astype(BF)

    def rep_first():
        @pl.when(rank < R - 1)
        def _():
            pl.semaphore_wait(ready, R - 1 - rank)

        for i in range(1, R):
            to = lax.rem(rep + i, R)
            push(("rs", i), term.at[pl.ds(pl.multiple_of(to * PIECE, PIECE), PIECE)], r_rep.at[i - 1], r_dev(i))

    def rep_sum():
        total = term[mine, :].astype(F32)
        arrive(("rs", 0), r_rep)
        for i in range(1, R):
            total += r_rep[i - 1].astype(F32)
        delta[mine, :] = total.astype(BF)
        for i in range(1, R):
            push(("ag", i), delta.at[mine], delta.at[mine], r_dev(i))

    def rep_final():
        arrive(("ag", 0), r_rep)
        loads["p"].wait()
        loads["m"].wait()
        step = delta[...].astype(F32) * (1.0 / R)
        moment = 0.9 * mv[...] + step
        mv[...] = moment
        pv[...] = pv[...] - 0.7 * (step + 0.9 * moment)
        load("po", pv, par_out)
        load("mo", mv, mom_out)

    def project(ks, first):
        for n, k in enumerate(ks):
            part = jnp.dot(abuf[yk(k)], wbuf[yk(k)].reshape(BLK, KV), preferred_element_type=F32)
            if first and n == 0:
                pacc[...] = part
            else:
                pacc[...] += part

    push(("c",), cot.at[0], cbuf.at[pl.ds(TOK, TOK)], z_dev)
    w1_first()
    w0_first()
    send_a(4)
    w1_to_x(0, wsh.at[0, rows1])
    dequantize()
    w1_step(1)
    w0_x_arrived()
    w1_step(2)
    loads["c"].wait()
    arrive(("c",), cbuf.at[pl.ds(TOK, TOK)])
    send_a(3)
    send_a(-3)
    weight_grad(4)
    send_a(2)
    g0_first()
    g1_to_x(4)
    w1_step(3)
    w0_step(1)
    w1_x_arrived(0)
    input_grad(0)
    pl.when(late)(rep_first)
    weight_grad(3)
    send_a(-2)
    weight_grad(-3)
    send_a(1)
    g0_step(1)
    g1_to_x(3)
    g1_to_x(-3)
    w1_step(4)
    w0_step(2)
    w1_x_arrived(-1)
    input_grad(-1)
    w1_x_arrived(1)
    input_grad(1)
    g1_first()
    weight_grad(2)
    send_a(-1)
    weight_grad(-2)
    send_a(0)
    pl.when(jnp.logical_not(late))(rep_first)
    g0_step(2)
    g1_to_x(2)
    g1_to_x(-2)
    w0_step(3)
    w1_x_arrived(-2)
    input_grad(-2)
    w1_x_arrived(2)
    input_grad(2)
    pl.when(late)(rep_sum)
    g1_step(1)
    weight_grad(1)
    weight_grad(-1)
    g0_step(3)
    g1_to_x(1)
    g1_to_x(-1)
    w1_x_arrived(-3)
    input_grad(-3)
    w1_x_arrived(3)
    input_grad(3)
    weight_grad(0)
    g1_to_x(0)
    g1_step(2)
    w0_step(4)
    w1_x_arrived(4)
    input_grad(4)
    project(ORDER, True)
    p_send[...] = pacc[TOK:].astype(BF)
    push(("p",), p_send, p_recv, z_dev)
    pl.when(jnp.logical_not(late))(rep_sum)
    g0_end()
    g1_step(3)
    rep_final()
    g0_final()
    g1_final()
    load("wo", wg_stage, wg_out.at[0])
    arrive(("p",), p_recv)
    p_stage[...] = (pacc[:TOK] + p_recv[...].astype(F32)).astype(BF)
    load("pr", p_stage, proj_out.at[0])
    arrive(("da", 0), da_far)
    steps = wbuf.at[pl.ds(0, 7), pl.ds(0, 2)]
    small = s1.at[pl.ds(0, 7)]
    for kind, ref in (
        ("c", p_recv), ("p", p_recv), ("a", da_far), ("da", da_far), ("w0x", x0), ("g0x", x0), ("w1x", x1), ("g1x", x1),
        ("w0y", steps), ("g0y", steps), ("w1y", small), ("g1y", small), ("rs", r_rep), ("ag", r_rep),
    ):
        sent(kind, ref)
    pltpu.make_async_copy(da_own, da_far, local.at[18]).wait()
    for key in ("po", "mo", "wo", "pr"):
        loads[key].wait()


def write_out(*refs):
    ins, outs, stages = refs[:5], refs[5:10], refs[10:15]
    in_sem, out_sem = refs[15:]
    step = TOK // 4
    parts = [(1, (0, pl.ds(i * step, step))) for i in range(4)] + [(n, (0,)) for n in (0, 2)]
    parts += [(n, (slice(None),)) for n in (3, 4)]
    there = [pltpu.make_async_copy(ins[n].at[p], stages[n].at[p], in_sem.at[i]) for i, (n, p) in enumerate(parts)]
    back = [pltpu.make_async_copy(stages[n].at[p], outs[n].at[p], out_sem.at[i]) for i, (n, p) in enumerate(parts)]
    for copy in there:
        copy.start()
    for first, second in zip(there, back):
        first.wait()
        second.start()
    for copy in back:
        copy.wait()


def body(activations, weight, cotangent, quantized, scales, outer_params, momentum):
    any_spec = pl.BlockSpec(memory_space=pl.ANY)
    vm = pltpu.VMEM
    out = pl.pallas_call(
        kernel,
        out_shape=(
            jax.ShapeDtypeStruct((1, TOK, KV), BF),
            jax.ShapeDtypeStruct((1, TOK, D), BF),
            jax.ShapeDtypeStruct((1, SHARD, KV), BF),
            jax.ShapeDtypeStruct((SIDE, SIDE), F32),
            jax.ShapeDtypeStruct((SIDE, SIDE), F32),
        ),
        in_specs=[any_spec] * 7,
        out_specs=[any_spec] * 5,
        scratch_shapes=[
            vm((Y, 2 * TOK, BLK), BF),
            vm((2 * TOK, KV), BF),
            vm((Y, X, SHARD, KV), BF),
            vm((Y, X, HROWS, KV), BF),
            vm((Y, X, HROWS, KV), BF),
            vm((2, 4, X, HROWS, KV), BF),
            vm((3, Y, HROWS, KV), BF),
            vm((Y, HROWS, KV), BF),
            vm((2, 4, HROWS, KV), BF),
            vm((3, HROWS, KV), BF),
            vm((Y, TOK, BLK), BF),
            vm((Y, TOK, BLK), BF),
            vm((TOK, KV), BF),
            vm((TOK, KV), BF),
            vm((TOK, KV), BF),
            vm((SHARD, KV), BF),
            vm((SIDE, SIDE), BF),
            vm((R - 1, PIECE, SIDE), BF),
            vm((SIDE, SIDE), BF),
            vm((SIDE, SIDE), jnp.int32),
            vm((1, SHARD), F32),
            vm((SIDE, SIDE), F32),
            vm((SIDE, SIDE), F32),
            vm((2 * TOK, KV), F32),
            pltpu.SemaphoreType.DMA((NSEND,)),
            pltpu.SemaphoreType.DMA((NRECV,)),
            pltpu.SemaphoreType.DMA((19,)),
            pltpu.SemaphoreType.REGULAR,
        ],
        compiler_params=pltpu.CompilerParams(
            collective_id=0, has_side_effects=True, vmem_limit_bytes=60 << 20),
        cost_estimate=pl.CostEstimate(
            flops=3 * 2 * TOK * D * KV, bytes_accessed=4 << 20, transcendentals=0),
    )(
        activations, weight, cotangent, quantized.reshape(SIDE, SIDE), scales,
        outer_params.reshape(SIDE, SIDE), momentum.reshape(SIDE, SIDE),
    )
    projected, input_grad, weight_grad, new_params, new_momentum = pl.pallas_call(
        write_out,
        out_shape=tuple(jax.ShapeDtypeStruct(a.shape, a.dtype) for a in out),
        in_specs=[any_spec] * 5,
        out_specs=[any_spec] * 5,
        scratch_shapes=[vm(a.shape, a.dtype) for a in out]
        + [pltpu.SemaphoreType.DMA((8,)), pltpu.SemaphoreType.DMA((8,))],
        compiler_params=pltpu.CompilerParams(vmem_limit_bytes=60 << 20),
    )(*out)
    return projected, input_grad, weight_grad, new_params.reshape(-1), new_momentum.reshape(-1)


def solution(mesh):
    placed = (
        P("replica", "fsdp", None),
        P("replica", "fsdp", None),
        P("replica", "fsdp", None),
        P("replica", "fsdp"),
        P("replica", "fsdp"),
        P("fsdp"),
        P("fsdp"),
    )
    return jax.shard_map(
        body,
        mesh=mesh,
        in_specs=placed,
        out_specs=(
            P("replica", "fsdp", None),
            P("replica", "fsdp", None),
            P("replica", "fsdp", None),
            P("fsdp"),
            P("fsdp"),
        ),
        check_vma=False,
    )
```

```python
import functools

import jax
import jax.numpy as jnp
from jax import lax
from jax.experimental import pallas as pl
from jax.experimental.pallas import tpu as pltpu
from jax.sharding import PartitionSpec as P

X, Y, Z, R = 4, 8, 2, 8
TOK, D, KV, SHARD = 128, 4096, 512, 64
HALF = D // Z
BLK = HALF // Y
HROWS = SHARD // 2
QROWS = HROWS // 2
SIDE = 128
PIECE = SIDE // R
NSEND, NRECV = 14, 80
ORDER = (4, 3, -3, 2, -2, 1, -1, 0)
BF, F32 = jnp.bfloat16, jnp.float32


def kernel(
    act, wsh, cot, quant, scale, par_in, mom_in,
    proj_out, ig_out, wg_out, par_out, mom_out,
    abuf, cbuf, wbuf, g0, g1, r0, x1, s1, r1, x0, da_own, da_far,
    p_send, p_recv, p_stage, wg_stage, term, r_rep, delta, qv, sv, pv, mv, pacc,
    send, recv, local, ready,
):
    rep = lax.axis_index("replica")
    me = lax.axis_index("fsdp")
    z = lax.div(me, X * Y)
    y = lax.rem(lax.div(me, X), Y)
    x = lax.rem(me, X)
    far = 1 - z

    def at(zz, yy, xx):
        return (rep, zz * (X * Y) + yy * X + xx)

    def yk(k):
        return lax.rem(y + (k + Y), Y)

    def xk(j):
        return lax.rem(x + (j + X), X)

    z_dev = at(far, y, x)
    y_dev = {1: at(z, yk(1), x), -1: at(z, yk(-1), x)}
    x_dev = {j: at(z, y, xk(j)) for j in (1, 2, 3)}

    def r_dev(i):
        return (lax.rem(rep + i, R), me)

    send_ids, recv_ids = {}, {}

    def together(key):
        return key[:-1] if key[0] in ("w1x", "g1x", "w0x", "g0x", "rs", "ag", "da") else key

    def remote(key, src, dst, dev):
        i = send_ids.setdefault(key[0], len(send_ids))
        j = recv_ids.setdefault(together(key), len(recv_ids))
        assert i < NSEND and j < NRECV, (i, j)
        return pltpu.make_async_remote_copy(
            src_ref=src, dst_ref=dst, send_sem=send.at[i], recv_sem=recv.at[j],
            device_id=dev, device_id_type=pl.DeviceIdType.MESH)

    def push(key, src, dst, dev):
        remote(key, src, dst, dev).start()

    def arrive(key, ref):
        remote(key, ref, ref, z_dev).wait_recv()

    def sent(kind, ref):
        pltpu.make_async_remote_copy(
            src_ref=ref, dst_ref=ref, send_sem=send.at[send_ids[kind]], recv_sem=recv.at[0],
            device_id=z_dev, device_id_type=pl.DeviceIdType.MESH).wait_send()

    loads = {}

    def load(key, src, dst):
        loads[key] = pltpu.make_async_copy(src, dst, local.at[len(loads)])
        loads[key].start()

    barrier = pltpu.get_barrier_semaphore()
    peers = [z_dev, y_dev[1], y_dev[-1]] + list(x_dev.values())

    def greet(sem_ref, dev):
        pl.semaphore_signal(sem_ref, inc=1, device_id=dev, device_id_type=pl.DeviceIdType.MESH)

    peers.append((rep + 1 - 2 * lax.rem(rep, 2), me))
    for dev in peers:
        greet(barrier, dev)

    slab = lax.div(rep, 2)
    slabs = R // 2
    late = slab >= slabs // 2

    def cols(zz, k):
        return pl.ds(pl.multiple_of(zz * HALF + yk(k) * BLK, BLK), BLK)

    load("q", quant, qv)
    load("s", scale, sv)
    load("w", wsh.at[0], wbuf.at[y, x])
    load("c", cot.at[0], cbuf.at[pl.ds(0, TOK)])
    for k in ORDER:
        load(("a", k), act.at[0, :, cols(z, k)], abuf.at[yk(k), pl.ds(0, TOK)])
    load("p", par_in, pv)
    load("m", mom_in, mv)

    pl.semaphore_wait(barrier, len(peers) + 2 * slab)

    def greet_slabs():
        for step in range(1, slabs):
            other = lax.rem(slab + step, slabs)

            @pl.when(other > slab)
            def _():
                for c in (0, 1):
                    greet(barrier, (other * 2 + c, me))

            @pl.when(other < slab)
            def _():
                for c in (0, 1):
                    greet(ready, (other * 2 + c, me))

    rows0 = pl.ds(0, HROWS)
    rows1 = pl.ds(HROWS, HROWS)
    quarter = {1: pl.ds(HROWS, QROWS), -1: pl.ds(HROWS + QROWS, QROWS)}
    half_of = {1: 0, -1: 1}

    def pair(h):
        return pl.ds(2 * h, 2)

    def send_a(k):
        push(("a", k), act.at[0, :, cols(far, k)], abuf.at[yk(k), pl.ds(TOK, TOK)], z_dev)

    def w1_first():
        for d in (1, -1):
            push(("w1y", d, 1), wsh.at[0, rows1], wbuf.at[y, x, rows1], y_dev[d])

    def w1_to_x(k, src):
        for j in (1, 3, 2):
            push(("w1x", k, j), src, wbuf.at[yk(k), x, rows1], x_dev[j])

    def w1_step(s):
        for d in (1, -1):
            k = -d * s
            if s < 4:
                ref = wbuf.at[yk(k), x, rows1]
                arrive(("w1y", d, s), ref)
                if s < 3:
                    push(("w1y", d, s + 1), ref, ref, y_dev[d])
                else:
                    part = wbuf.at[yk(k), x, quarter[d]]
                    push(("w1y", d, 4), part, part, y_dev[d])
            else:
                arrive(("w1y", d, 4), wbuf.at[yk(4), x, quarter[d]])
        for k in ((-s, s) if s < 4 else (4,)):
            w1_to_x(k, wbuf.at[yk(k), x, rows1])

    def w0_first():
        for j in (1, 3, 2):
            push(("w0x", j), wsh.at[0, rows0], wbuf.at[y, x, rows0], x_dev[j])

    def w0_row(k, h):
        return wbuf.at[yk(k), pair(h), rows0]

    def w0_x_arrived():
        arrive(("w0x", 0), x0)
        loads["w"].wait()
        for h in (0, 1):
            for d in (1, -1):
                push(("w0y", d, 1, h), w0_row(0, h), w0_row(0, h), y_dev[d])

    def w0_step(s):
        for h in (0, 1):
            for d in (1, -1):
                k = -d * s
                if s < 4:
                    ref = w0_row(k, h)
                    arrive(("w0y", d, s, h), ref)
                    if s < 3 or half_of[d] == h:
                        push(("w0y", d, s + 1, h), ref, ref, y_dev[d])
                elif half_of[d] == h:
                    arrive(("w0y", d, 4, h), w0_row(4, h))

    def w1_x_arrived(k):
        arrive(("w1x", k, 0), x0)

    def input_grad(k):
        w = wbuf[yk(k)].reshape(BLK, KV)
        out = lax.dot_general(cbuf[...], w, (((1,), (1,)), ((), ())),
                              preferred_element_type=F32).astype(BF)
        da_far[yk(k)] = out[TOK:]
        push(("da", k), da_far.at[yk(k)], ig_out.at[0, :, cols(z, k)], z_dev)
        da_own[yk(k)] = out[:TOK]
        pltpu.make_async_copy(da_own.at[yk(k)], ig_out.at[0, :, cols(z, k)], local.at[18]).start()

    def weight_grad(k):
        loads["a", k].wait()
        arrive(("a", k), abuf.at[yk(k), pl.ds(TOK, TOK)])
        g = lax.dot_general(abuf[yk(k)], cbuf[...], (((0,), (0,)), ((), ())),
                            preferred_element_type=F32).astype(BF)
        g = g.reshape(X, SHARD, KV)
        g0[yk(k)] = g[:, :HROWS]
        g1[yk(k)] = g[:, HROWS:]

    def g0_send(s, d, h, k):
        ref = g0.at[yk(k), pair(h)]
        push(("g0y", d, s, h), ref, r0.at[half_of[d], s - 1, pair(h)], y_dev[d])

    def g0_first():
        for d in (1, -1):
            g0_send(1, d, half_of[d], 4)

    def g0_step(s):
        for d in (1, -1):
            k = d * (4 - s)
            for h in (0, 1):
                if s > 1 or half_of[d] == h:
                    slot = r0.at[half_of[d], s - 1, pair(h)]
                    arrive(("g0y", d, s, h), slot)
                    own = g0.at[yk(k), pair(h)]
                    own[...] = (own[...].astype(F32) + slot[...].astype(F32)).astype(BF)
                g0_send(s + 1, d, h, k)

    def g0_end():
        for d in (1, -1):
            for h in (0, 1):
                arrive(("g0y", d, 4, h), r0.at[half_of[d], 3, pair(h)])
        g0[y] = (g0[y].astype(F32) + r0[0, 3].astype(F32) + r0[1, 3].astype(F32)).astype(BF)
        for j in (1, 3, 2):
            push(("g0x", j), g0.at[y, xk(j)], x0.at[j - 1], x_dev[j])

    def g0_final():
        total = g0[y, x].astype(F32)
        arrive(("g0x", 0), x0)
        for j in (1, 3, 2):
            total += x0[j - 1].astype(F32)
        wg_stage[0:HROWS] = total.astype(BF)

    def g1_to_x(k):
        for j in (1, 3, 2):
            push(("g1x", k, j), g1.at[yk(k), xk(j)], x1.at[j - 1, yk(k)], x_dev[j])

    def g1_from_x(k):
        total = g1[yk(k), x].astype(F32)
        arrive(("g1x", k, 0), x0)
        for j in (1, 3, 2):
            total += x1[j - 1, yk(k)].astype(F32)
        return total

    g_quarter = {1: pl.ds(0, QROWS), -1: pl.ds(QROWS, QROWS)}

    def g1_first():
        s1[yk(4)] = g1_from_x(4).astype(BF)
        for d in (1, -1):
            push(("g1y", d, 1), s1.at[yk(4), g_quarter[d]], r1.at[half_of[d], 0, g_quarter[d]], y_dev[d])

    def g1_step(s):
        for d in (1, -1):
            k = d * (4 - s)
            total = g1_from_x(k)
            if s == 1:
                slot = r1.at[half_of[d], 0, g_quarter[d]]
                arrive(("g1y", d, 1), slot)
                got = slot[...].astype(F32)
                parts = [total[:QROWS], total[QROWS:]]
                parts[half_of[d]] += got
                s1[yk(k), 0:QROWS] = parts[0].astype(BF)
                s1[yk(k), QROWS:HROWS] = parts[1].astype(BF)
            else:
                slot = r1.at[half_of[d], s - 1]
                arrive(("g1y", d, s), slot)
                s1[yk(k)] = (total + slot[...].astype(F32)).astype(BF)
            push(("g1y", d, s + 1), s1.at[yk(k)], r1.at[half_of[d], s], y_dev[d])

    def g1_final():
        total = g1_from_x(0)
        for d in (1, -1):
            arrive(("g1y", d, 4), r1.at[half_of[d], 3])
            total += r1[half_of[d], 3].astype(F32)
        wg_stage[HROWS:SHARD] = total.astype(BF)

    mine = pl.ds(pl.multiple_of(rep * PIECE, PIECE), PIECE)

    def dequantize():
        loads["q"].wait()
        loads["s"].wait()
        owner = lax.broadcasted_iota(jnp.int32, (SIDE, SHARD), 0) // 2
        lane = lax.broadcasted_iota(jnp.int32, (SIDE, SHARD), 1)
        row_scale = jnp.sum(jnp.where(owner == lane, sv[...], 0.0), axis=1, keepdims=True)
        term[...] = (qv[...].astype(F32) * row_scale).astype(BF)

    def rep_first():
        @pl.when(slab < slabs - 1)
        def _():
            pl.semaphore_wait(ready, 2 * (slabs - 1 - slab))

        for i in range(1, R):
            to = lax.rem(rep + i, R)
            push(("rs", i), term.at[pl.ds(pl.multiple_of(to * PIECE, PIECE), PIECE)], r_rep.at[i - 1], r_dev(i))

    def rep_sum():
        total = term[mine, :].astype(F32)
        arrive(("rs", 0), r_rep)
        for i in range(1, R):
            total += r_rep[i - 1].astype(F32)
        delta[mine, :] = total.astype(BF)
        for i in range(1, R):
            push(("ag", i), delta.at[mine], delta.at[mine], r_dev(i))

    def rep_final():
        arrive(("ag", 0), r_rep)
        loads["p"].wait()
        loads["m"].wait()
        step = delta[...].astype(F32) * (1.0 / R)
        moment = 0.9 * mv[...] + step
        mv[...] = moment
        pv[...] = pv[...] - 0.7 * (step + 0.9 * moment)
        load("po", pv, par_out)
        load("mo", mv, mom_out)

    def project(ks, first):
        rows = jnp.concatenate([abuf[yk(k)] for k in ks], axis=1)
        matrix = jnp.concatenate([wbuf[yk(k)].reshape(BLK, KV) for k in ks], axis=0)
        part = jnp.dot(rows, matrix, preferred_element_type=F32)
        pacc[...] = part if first else pacc[...] + part

    push(("c",), cot.at[0], cbuf.at[pl.ds(TOK, TOK)], z_dev)
    w1_first()
    w0_first()
    send_a(4)
    w1_to_x(0, wsh.at[0, rows1])
    greet_slabs()
    dequantize()
    w1_step(1)
    w0_x_arrived()
    w1_step(2)
    loads["c"].wait()
    arrive(("c",), cbuf.at[pl.ds(TOK, TOK)])
    send_a(3)
    send_a(-3)
    weight_grad(4)
    send_a(2)
    g0_first()
    g1_to_x(4)
    w1_step(3)
    w0_step(1)
    w1_x_arrived(0)
    input_grad(0)
    pl.when(late)(rep_first)
    weight_grad(3)
    send_a(-2)
    weight_grad(-3)
    send_a(1)
    g0_step(1)
    g1_to_x(3)
    g1_to_x(-3)
    w1_step(4)
    w0_step(2)
    w1_x_arrived(-1)
    input_grad(-1)
    w1_x_arrived(1)
    input_grad(1)
    g1_first()
    weight_grad(2)
    send_a(-1)
    weight_grad(-2)
    send_a(0)
    pl.when(jnp.logical_not(late))(rep_first)
    g0_step(2)
    g1_to_x(2)
    g1_to_x(-2)
    pl.when(late)(rep_sum)
    w0_step(3)
    w1_x_arrived(-2)
    input_grad(-2)
    w1_x_arrived(2)
    input_grad(2)
    g1_step(1)
    weight_grad(1)
    weight_grad(-1)
    g0_step(3)
    g1_to_x(1)
    g1_to_x(-1)
    w1_x_arrived(-3)
    input_grad(-3)
    w1_x_arrived(3)
    input_grad(3)
    weight_grad(0)
    g1_to_x(0)
    g1_step(2)
    project((0, 1, -1, 2, -2), True)
    w0_step(4)
    w1_x_arrived(4)
    project((3, -3, 4), False)
    p_send[...] = pacc[TOK:].astype(BF)
    push(("p",), p_send, p_recv, z_dev)
    input_grad(4)
    pl.when(jnp.logical_not(late))(rep_sum)
    g0_end()
    g1_step(3)
    rep_final()
    g0_final()
    g1_final()
    load("wo", wg_stage, wg_out.at[0])
    arrive(("p",), p_recv)
    p_stage[...] = (pacc[:TOK] + p_recv[...].astype(F32)).astype(BF)
    load("pr", p_stage, proj_out.at[0])
    arrive(("da", 0), da_far)
    steps = wbuf.at[pl.ds(0, 7), pl.ds(0, 2)]
    small = s1.at[pl.ds(0, 7)]
    for kind, ref in (
        ("c", p_recv), ("p", p_recv), ("a", da_far), ("da", da_far), ("w0x", x0), ("g0x", x0), ("w1x", x1), ("g1x", x1),
        ("w0y", steps), ("g0y", steps), ("w1y", small), ("g1y", small), ("rs", r_rep), ("ag", r_rep),
    ):
        sent(kind, ref)
    pltpu.make_async_copy(da_own, da_far, local.at[18]).wait()
    for key in ("po", "mo", "wo", "pr"):
        loads[key].wait()


def write_out(*refs):
    ins, outs, stages = refs[:5], refs[5:10], refs[10:15]
    in_sem, out_sem = refs[15:]
    step = TOK // 4
    parts = [(1, (0, pl.ds(i * step, step))) for i in range(4)] + [(n, (0,)) for n in (0, 2)]
    parts += [(n, (slice(None),)) for n in (3, 4)]
    there = [pltpu.make_async_copy(ins[n].at[p], stages[n].at[p], in_sem.at[i]) for i, (n, p) in enumerate(parts)]
    back = [pltpu.make_async_copy(stages[n].at[p], outs[n].at[p], out_sem.at[i]) for i, (n, p) in enumerate(parts)]
    for copy in there:
        copy.start()
    for first, second in zip(there, back):
        first.wait()
        second.start()
    for copy in back:
        copy.wait()


def body(activations, weight, cotangent, quantized, scales, outer_params, momentum):
    any_spec = pl.BlockSpec(memory_space=pl.ANY)
    vm = pltpu.VMEM
    out = pl.pallas_call(
        kernel,
        out_shape=(
            jax.ShapeDtypeStruct((1, TOK, KV), BF),
            jax.ShapeDtypeStruct((1, TOK, D), BF),
            jax.ShapeDtypeStruct((1, SHARD, KV), BF),
            jax.ShapeDtypeStruct((SIDE, SIDE), F32),
            jax.ShapeDtypeStruct((SIDE, SIDE), F32),
        ),
        in_specs=[any_spec] * 7,
        out_specs=[any_spec] * 5,
        scratch_shapes=[
            vm((Y, 2 * TOK, BLK), BF),
            vm((2 * TOK, KV), BF),
            vm((Y, X, SHARD, KV), BF),
            vm((Y, X, HROWS, KV), BF),
            vm((Y, X, HROWS, KV), BF),
            vm((2, 4, X, HROWS, KV), BF),
            vm((3, Y, HROWS, KV), BF),
            vm((Y, HROWS, KV), BF),
            vm((2, 4, HROWS, KV), BF),
            vm((3, HROWS, KV), BF),
            vm((Y, TOK, BLK), BF),
            vm((Y, TOK, BLK), BF),
            vm((TOK, KV), BF),
            vm((TOK, KV), BF),
            vm((TOK, KV), BF),
            vm((SHARD, KV), BF),
            vm((SIDE, SIDE), BF),
            vm((R - 1, PIECE, SIDE), BF),
            vm((SIDE, SIDE), BF),
            vm((SIDE, SIDE), jnp.int32),
            vm((1, SHARD), F32),
            vm((SIDE, SIDE), F32),
            vm((SIDE, SIDE), F32),
            vm((2 * TOK, KV), F32),
            pltpu.SemaphoreType.DMA((NSEND,)),
            pltpu.SemaphoreType.DMA((NRECV,)),
            pltpu.SemaphoreType.DMA((19,)),
            pltpu.SemaphoreType.REGULAR,
        ],
        compiler_params=pltpu.CompilerParams(
            collective_id=0, has_side_effects=True, vmem_limit_bytes=60 << 20),
        cost_estimate=pl.CostEstimate(
            flops=3 * 2 * TOK * D * KV, bytes_accessed=4 << 20, transcendentals=0),
    )(
        activations, weight, cotangent, quantized.reshape(SIDE, SIDE), scales,
        outer_params.reshape(SIDE, SIDE), momentum.reshape(SIDE, SIDE),
    )
    projected, input_grad, weight_grad, new_params, new_momentum = pl.pallas_call(
        write_out,
        out_shape=tuple(jax.ShapeDtypeStruct(a.shape, a.dtype) for a in out),
        in_specs=[any_spec] * 5,
        out_specs=[any_spec] * 5,
        scratch_shapes=[vm(a.shape, a.dtype) for a in out]
        + [pltpu.SemaphoreType.DMA((8,)), pltpu.SemaphoreType.DMA((8,))],
        compiler_params=pltpu.CompilerParams(vmem_limit_bytes=60 << 20),
    )(*out)
    return projected, input_grad, weight_grad, new_params.reshape(-1), new_momentum.reshape(-1)


def solution(mesh):
    placed = (
        P("replica", "fsdp", None),
        P("replica", "fsdp", None),
        P("replica", "fsdp", None),
        P("replica", "fsdp"),
        P("replica", "fsdp"),
        P("fsdp"),
        P("fsdp"),
    )
    return jax.shard_map(
        body,
        mesh=mesh,
        in_specs=placed,
        out_specs=(
            P("replica", "fsdp", None),
            P("replica", "fsdp", None),
            P("replica", "fsdp", None),
            P("fsdp"),
            P("fsdp"),
        ),
        check_vma=False,
    )
```

```python
import functools

import jax
import jax.numpy as jnp
from jax import lax
from jax.experimental import pallas as pl
from jax.experimental.pallas import tpu as pltpu
from jax.sharding import PartitionSpec as P

X, Y, Z, R = 4, 8, 2, 8
TOK, D, KV, SHARD = 128, 4096, 512, 64
HALF = D // Z
BLK = HALF // Y
HROWS = SHARD // 2
QROWS = HROWS // 2
SIDE = 128
PIECE = SIDE // R
NSEND, NRECV = 14, 80
ORDER = (4, 3, -3, 2, -2, 1, -1, 0)
BF, F32 = jnp.bfloat16, jnp.float32


def kernel(
    act, wsh, cot, quant, scale, par_in, mom_in,
    proj_out, ig_out, wg_out, par_out, mom_out,
    abuf, cbuf, wbuf, g0, g1, r0, x1, s1, r1, x0, da_own, da_far,
    p_send, p_recv, p_stage, wg_stage, term, r_rep, delta, qv, sv, pv, mv, pacc,
    send, recv, local, ready,
):
    rep = lax.axis_index("replica")
    me = lax.axis_index("fsdp")
    z = lax.div(me, X * Y)
    y = lax.rem(lax.div(me, X), Y)
    x = lax.rem(me, X)
    far = 1 - z

    def at(zz, yy, xx):
        return (rep, zz * (X * Y) + yy * X + xx)

    def yk(k):
        return lax.rem(y + (k + Y), Y)

    def xk(j):
        return lax.rem(x + (j + X), X)

    z_dev = at(far, y, x)
    y_dev = {1: at(z, yk(1), x), -1: at(z, yk(-1), x)}
    x_dev = {j: at(z, y, xk(j)) for j in (1, 2, 3)}

    def r_dev(i):
        return (lax.rem(rep + i, R), me)

    send_ids, recv_ids = {}, {}

    def together(key):
        return key[:-1] if key[0] in ("w1x", "g1x", "w0x", "g0x", "rs", "ag", "da") else key

    def remote(key, src, dst, dev):
        i = send_ids.setdefault(key[0], len(send_ids))
        j = recv_ids.setdefault(together(key), len(recv_ids))
        assert i < NSEND and j < NRECV, (i, j)
        return pltpu.make_async_remote_copy(
            src_ref=src, dst_ref=dst, send_sem=send.at[i], recv_sem=recv.at[j],
            device_id=dev, device_id_type=pl.DeviceIdType.MESH)

    def push(key, src, dst, dev):
        remote(key, src, dst, dev).start()

    def arrive(key, ref):
        remote(key, ref, ref, z_dev).wait_recv()

    def sent(kind, ref):
        pltpu.make_async_remote_copy(
            src_ref=ref, dst_ref=ref, send_sem=send.at[send_ids[kind]], recv_sem=recv.at[0],
            device_id=z_dev, device_id_type=pl.DeviceIdType.MESH).wait_send()

    loads = {}

    def load(key, src, dst):
        loads[key] = pltpu.make_async_copy(src, dst, local.at[len(loads)])
        loads[key].start()

    barrier = pltpu.get_barrier_semaphore()
    peers = [z_dev, y_dev[1], y_dev[-1]] + list(x_dev.values())

    def greet(sem_ref, dev):
        pl.semaphore_signal(sem_ref, inc=1, device_id=dev, device_id_type=pl.DeviceIdType.MESH)

    peers.append((rep + 1 - 2 * lax.rem(rep, 2), me))
    for dev in peers:
        greet(barrier, dev)

    slab = lax.div(rep, 2)
    slabs = R // 2
    late = slab >= slabs // 2

    def cols(zz, k):
        return pl.ds(pl.multiple_of(zz * HALF + yk(k) * BLK, BLK), BLK)

    load("q", quant, qv)
    load("s", scale, sv)
    load("w", wsh.at[0], wbuf.at[y, x])
    load("c", cot.at[0], cbuf.at[pl.ds(0, TOK)])
    for k in ORDER:
        pltpu.make_async_copy(act.at[0, :, cols(z, k)], abuf.at[yk(k), pl.ds(0, TOK)], local.at[10]).start()
    load("p", par_in, pv)
    load("m", mom_in, mv)

    pl.semaphore_wait(barrier, len(peers) + 2 * slab)

    def greet_slabs():
        for step in range(1, slabs):
            other = lax.rem(slab + step, slabs)

            @pl.when(other > slab)
            def _():
                for c in (0, 1):
                    greet(barrier, (other * 2 + c, me))

            @pl.when(other < slab)
            def _():
                for c in (0, 1):
                    greet(ready, (other * 2 + c, me))

    rows0 = pl.ds(0, HROWS)
    rows1 = pl.ds(HROWS, HROWS)
    quarter = {1: pl.ds(HROWS, QROWS), -1: pl.ds(HROWS + QROWS, QROWS)}
    half_of = {1: 0, -1: 1}

    def pair(h):
        return pl.ds(2 * h, 2)

    def send_a(k):
        push(("a", k), act.at[0, :, cols(far, k)], abuf.at[yk(k), pl.ds(TOK, TOK)], z_dev)

    def w1_first():
        for d in (1, -1):
            push(("w1y", d, 1), wsh.at[0, rows1], wbuf.at[y, x, rows1], y_dev[d])

    def w1_to_x(k, src):
        for j in (1, 3, 2):
            push(("w1x", k, j), src, wbuf.at[yk(k), x, rows1], x_dev[j])

    def w1_step(s):
        for d in (1, -1):
            k = -d * s
            if s < 4:
                ref = wbuf.at[yk(k), x, rows1]
                arrive(("w1y", d, s), ref)
                if s < 3:
                    push(("w1y", d, s + 1), ref, ref, y_dev[d])
                else:
                    part = wbuf.at[yk(k), x, quarter[d]]
                    push(("w1y", d, 4), part, part, y_dev[d])
            else:
                arrive(("w1y", d, 4), wbuf.at[yk(4), x, quarter[d]])
        for k in ((-s, s) if s < 4 else (4,)):
            w1_to_x(k, wbuf.at[yk(k), x, rows1])

    def w0_first():
        for j in (1, 3, 2):
            push(("w0x", j), wsh.at[0, rows0], wbuf.at[y, x, rows0], x_dev[j])

    def w0_row(k, h):
        return wbuf.at[yk(k), pair(h), rows0]

    def w0_x_arrived():
        arrive(("w0x", 0), x0)
        loads["w"].wait()
        for h in (0, 1):
            for d in (1, -1):
                push(("w0y", d, 1, h), w0_row(0, h), w0_row(0, h), y_dev[d])

    def w0_step(s):
        for h in (0, 1):
            for d in (1, -1):
                k = -d * s
                if s < 4:
                    ref = w0_row(k, h)
                    arrive(("w0y", d, s, h), ref)
                    if s < 3 or half_of[d] == h:
                        push(("w0y", d, s + 1, h), ref, ref, y_dev[d])
                elif half_of[d] == h:
                    arrive(("w0y", d, 4, h), w0_row(4, h))

    def w1_x_arrived(k):
        arrive(("w1x", k, 0), x0)

    def input_grad(k):
        w = wbuf[yk(k)].reshape(BLK, KV)
        out = lax.dot_general(cbuf[...], w, (((1,), (1,)), ((), ())),
                              preferred_element_type=F32).astype(BF)
        da_far[yk(k)] = out[TOK:]
        push(("da", k), da_far.at[yk(k)], ig_out.at[0, :, cols(z, k)], z_dev)
        da_own[yk(k)] = out[:TOK]
        pltpu.make_async_copy(da_own.at[yk(k)], ig_out.at[0, :, cols(z, k)], local.at[11]).start()

    def weight_grad(k):
        if k == ORDER[0]:
            pltpu.make_async_copy(da_own, da_far, local.at[10]).wait()
        arrive(("a", k), abuf.at[yk(k), pl.ds(TOK, TOK)])
        g = lax.dot_general(abuf[yk(k)], cbuf[...], (((0,), (0,)), ((), ())),
                            preferred_element_type=F32).astype(BF)
        g = g.reshape(X, SHARD, KV)
        g0[yk(k)] = g[:, :HROWS]
        g1[yk(k)] = g[:, HROWS:]

    def g0_send(s, d, h, k):
        ref = g0.at[yk(k), pair(h)]
        push(("g0y", d, s, h), ref, r0.at[half_of[d], s - 1, pair(h)], y_dev[d])

    def g0_first():
        for d in (1, -1):
            g0_send(1, d, half_of[d], 4)

    def g0_step(s):
        for d in (1, -1):
            k = d * (4 - s)
            for h in (0, 1):
                if s > 1 or half_of[d] == h:
                    slot = r0.at[half_of[d], s - 1, pair(h)]
                    arrive(("g0y", d, s, h), slot)
                    own = g0.at[yk(k), pair(h)]
                    own[...] = (own[...].astype(F32) + slot[...].astype(F32)).astype(BF)
                g0_send(s + 1, d, h, k)

    def g0_end():
        for d in (1, -1):
            for h in (0, 1):
                arrive(("g0y", d, 4, h), r0.at[half_of[d], 3, pair(h)])
        g0[y] = (g0[y].astype(F32) + r0[0, 3].astype(F32) + r0[1, 3].astype(F32)).astype(BF)
        for j in (1, 3, 2):
            push(("g0x", j), g0.at[y, xk(j)], x0.at[j - 1], x_dev[j])

    def g0_final():
        total = g0[y, x].astype(F32)
        arrive(("g0x", 0), x0)
        for j in (1, 3, 2):
            total += x0[j - 1].astype(F32)
        wg_stage[0:HROWS] = total.astype(BF)

    def g1_to_x(k):
        for j in (1, 3, 2):
            push(("g1x", k, j), g1.at[yk(k), xk(j)], x1.at[j - 1, yk(k)], x_dev[j])

    def g1_from_x(k):
        total = g1[yk(k), x].astype(F32)
        arrive(("g1x", k, 0), x0)
        for j in (1, 3, 2):
            total += x1[j - 1, yk(k)].astype(F32)
        return total

    g_quarter = {1: pl.ds(0, QROWS), -1: pl.ds(QROWS, QROWS)}

    def g1_first():
        s1[yk(4)] = g1_from_x(4).astype(BF)
        for d in (1, -1):
            push(("g1y", d, 1), s1.at[yk(4), g_quarter[d]], r1.at[half_of[d], 0, g_quarter[d]], y_dev[d])

    def g1_step(s):
        for d in (1, -1):
            k = d * (4 - s)
            total = g1_from_x(k)
            if s == 1:
                slot = r1.at[half_of[d], 0, g_quarter[d]]
                arrive(("g1y", d, 1), slot)
                got = slot[...].astype(F32)
                parts = [total[:QROWS], total[QROWS:]]
                parts[half_of[d]] += got
                s1[yk(k), 0:QROWS] = parts[0].astype(BF)
                s1[yk(k), QROWS:HROWS] = parts[1].astype(BF)
            else:
                slot = r1.at[half_of[d], s - 1]
                arrive(("g1y", d, s), slot)
                s1[yk(k)] = (total + slot[...].astype(F32)).astype(BF)
            push(("g1y", d, s + 1), s1.at[yk(k)], r1.at[half_of[d], s], y_dev[d])

    def g1_final():
        total = g1_from_x(0)
        for d in (1, -1):
            arrive(("g1y", d, 4), r1.at[half_of[d], 3])
            total += r1[half_of[d], 3].astype(F32)
        wg_stage[HROWS:SHARD] = total.astype(BF)

    mine = pl.ds(pl.multiple_of(rep * PIECE, PIECE), PIECE)

    def dequantize():
        loads["q"].wait()
        loads["s"].wait()
        owner = lax.broadcasted_iota(jnp.int32, (SIDE, SHARD), 0) // 2
        lane = lax.broadcasted_iota(jnp.int32, (SIDE, SHARD), 1)
        row_scale = jnp.sum(jnp.where(owner == lane, sv[...], 0.0), axis=1, keepdims=True)
        term[...] = (qv[...].astype(F32) * row_scale).astype(BF)

    def rep_first():
        @pl.when(slab < slabs - 1)
        def _():
            pl.semaphore_wait(ready, 2 * (slabs - 1 - slab))

        for i in range(1, R):
            to = lax.rem(rep + i, R)
            push(("rs", i), term.at[pl.ds(pl.multiple_of(to * PIECE, PIECE), PIECE)], r_rep.at[i - 1], r_dev(i))

    def rep_sum():
        total = term[mine, :].astype(F32)
        arrive(("rs", 0), r_rep)
        for i in range(1, R):
            total += r_rep[i - 1].astype(F32)
        delta[mine, :] = total.astype(BF)
        for i in range(1, R):
            push(("ag", i), delta.at[mine], delta.at[mine], r_dev(i))

    def rep_final():
        arrive(("ag", 0), r_rep)
        loads["p"].wait()
        loads["m"].wait()
        step = delta[...].astype(F32) * (1.0 / R)
        moment = 0.9 * mv[...] + step
        mv[...] = moment
        pv[...] = pv[...] - 0.7 * (step + 0.9 * moment)
        load("po", pv, par_out)
        load("mo", mv, mom_out)

    def project(ks, first):
        rows = jnp.concatenate([abuf[yk(k)] for k in ks], axis=1)
        matrix = jnp.concatenate([wbuf[yk(k)].reshape(BLK, KV) for k in ks], axis=0)
        part = jnp.dot(rows, matrix, preferred_element_type=F32)
        pacc[...] = part if first else pacc[...] + part

    push(("c",), cot.at[0], cbuf.at[pl.ds(TOK, TOK)], z_dev)
    w1_first()
    w0_first()
    send_a(4)
    w1_to_x(0, wsh.at[0, rows1])
    greet_slabs()
    dequantize()
    w1_step(1)
    w0_x_arrived()
    w1_step(2)
    loads["c"].wait()
    arrive(("c",), cbuf.at[pl.ds(TOK, TOK)])
    send_a(3)
    send_a(-3)
    weight_grad(4)
    send_a(2)
    g0_first()
    g1_to_x(4)
    w1_step(3)
    w0_step(1)
    w1_x_arrived(0)
    input_grad(0)
    pl.when(late)(rep_first)
    weight_grad(3)
    send_a(-2)
    weight_grad(-3)
    send_a(1)
    g0_step(1)
    g1_to_x(3)
    g1_to_x(-3)
    w1_step(4)
    w0_step(2)
    w1_x_arrived(-1)
    input_grad(-1)
    w1_x_arrived(1)
    input_grad(1)
    g1_first()
    weight_grad(2)
    send_a(-1)
    weight_grad(-2)
    send_a(0)
    pl.when(jnp.logical_not(late))(rep_first)
    g0_step(2)
    g1_to_x(2)
    g1_to_x(-2)
    pl.when(late)(rep_sum)
    w0_step(3)
    w1_x_arrived(-2)
    input_grad(-2)
    w1_x_arrived(2)
    input_grad(2)
    g1_step(1)
    weight_grad(1)
    weight_grad(-1)
    g0_step(3)
    g1_to_x(1)
    g1_to_x(-1)
    w1_x_arrived(-3)
    input_grad(-3)
    w1_x_arrived(3)
    input_grad(3)
    weight_grad(0)
    g1_to_x(0)
    g1_step(2)
    project((0, 1, -1, 2, -2), True)
    w0_step(4)
    w1_x_arrived(4)
    project((3, -3, 4), False)
    p_send[...] = pacc[TOK:].astype(BF)
    push(("p",), p_send, p_recv, z_dev)
    input_grad(4)
    pl.when(jnp.logical_not(late))(rep_sum)
    g0_end()
    g1_step(3)
    rep_final()
    g0_final()
    g1_final()
    load("wo", wg_stage, wg_out.at[0])
    arrive(("p",), p_recv)
    p_stage[...] = (pacc[:TOK] + p_recv[...].astype(F32)).astype(BF)
    load("pr", p_stage, proj_out.at[0])
    arrive(("da", 0), da_far)
    steps = wbuf.at[pl.ds(0, 7), pl.ds(0, 2)]
    small = s1.at[pl.ds(0, 7)]
    for kind, ref in (
        ("c", p_recv), ("p", p_recv), ("a", da_far), ("da", da_far), ("w0x", x0), ("g0x", x0), ("w1x", x1), ("g1x", x1),
        ("w0y", steps), ("g0y", steps), ("w1y", small), ("g1y", small), ("rs", r_rep), ("ag", r_rep),
    ):
        sent(kind, ref)
    pltpu.make_async_copy(da_own, da_far, local.at[11]).wait()
    for key in ("po", "mo", "wo", "pr"):
        loads[key].wait()


def write_out(*refs):
    ins, outs, stages = refs[:5], refs[5:10], refs[10:15]
    in_sem, out_sem = refs[15:]
    step = TOK // 8
    parts = [(1, (0, pl.ds(i * step, step))) for i in range(8)] + [(n, (0,)) for n in (0, 2)]
    parts += [(n, (slice(None),)) for n in (3, 4)]
    there = [pltpu.make_async_copy(ins[n].at[p], stages[n].at[p], in_sem.at[i]) for i, (n, p) in enumerate(parts)]
    back = [pltpu.make_async_copy(stages[n].at[p], outs[n].at[p], out_sem.at[i]) for i, (n, p) in enumerate(parts)]
    for copy in there:
        copy.start()
    for first, second in zip(there, back):
        first.wait()
        second.start()
    for copy in back:
        copy.wait()


def body(activations, weight, cotangent, quantized, scales, outer_params, momentum):
    any_spec = pl.BlockSpec(memory_space=pl.ANY)
    vm = pltpu.VMEM
    out = pl.pallas_call(
        kernel,
        out_shape=(
            jax.ShapeDtypeStruct((1, TOK, KV), BF),
            jax.ShapeDtypeStruct((1, TOK, D), BF),
            jax.ShapeDtypeStruct((1, SHARD, KV), BF),
            jax.ShapeDtypeStruct((SIDE, SIDE), F32),
            jax.ShapeDtypeStruct((SIDE, SIDE), F32),
        ),
        in_specs=[any_spec] * 7,
        out_specs=[any_spec] * 5,
        scratch_shapes=[
            vm((Y, 2 * TOK, BLK), BF),
            vm((2 * TOK, KV), BF),
            vm((Y, X, SHARD, KV), BF),
            vm((Y, X, HROWS, KV), BF),
            vm((Y, X, HROWS, KV), BF),
            vm((2, 4, X, HROWS, KV), BF),
            vm((3, Y, HROWS, KV), BF),
            vm((Y, HROWS, KV), BF),
            vm((2, 4, HROWS, KV), BF),
            vm((3, HROWS, KV), BF),
            vm((Y, TOK, BLK), BF),
            vm((Y, TOK, BLK), BF),
            vm((TOK, KV), BF),
            vm((TOK, KV), BF),
            vm((TOK, KV), BF),
            vm((SHARD, KV), BF),
            vm((SIDE, SIDE), BF),
            vm((R - 1, PIECE, SIDE), BF),
            vm((SIDE, SIDE), BF),
            vm((SIDE, SIDE), jnp.int32),
            vm((1, SHARD), F32),
            vm((SIDE, SIDE), F32),
            vm((SIDE, SIDE), F32),
            vm((2 * TOK, KV), F32),
            pltpu.SemaphoreType.DMA((NSEND,)),
            pltpu.SemaphoreType.DMA((NRECV,)),
            pltpu.SemaphoreType.DMA((12,)),
            pltpu.SemaphoreType.REGULAR,
        ],
        compiler_params=pltpu.CompilerParams(
            collective_id=0, has_side_effects=True, vmem_limit_bytes=60 << 20),
        cost_estimate=pl.CostEstimate(
            flops=3 * 2 * TOK * D * KV, bytes_accessed=4 << 20, transcendentals=0),
    )(
        activations, weight, cotangent, quantized.reshape(SIDE, SIDE), scales,
        outer_params.reshape(SIDE, SIDE), momentum.reshape(SIDE, SIDE),
    )
    projected, input_grad, weight_grad, new_params, new_momentum = pl.pallas_call(
        write_out,
        out_shape=tuple(jax.ShapeDtypeStruct(a.shape, a.dtype) for a in out),
        in_specs=[any_spec] * 5,
        out_specs=[any_spec] * 5,
        scratch_shapes=[vm(a.shape, a.dtype) for a in out]
        + [pltpu.SemaphoreType.DMA((12,)), pltpu.SemaphoreType.DMA((12,))],
        compiler_params=pltpu.CompilerParams(vmem_limit_bytes=60 << 20),
    )(*out)
    return projected, input_grad, weight_grad, new_params.reshape(-1), new_momentum.reshape(-1)


def solution(mesh):
    placed = (
        P("replica", "fsdp", None),
        P("replica", "fsdp", None),
        P("replica", "fsdp", None),
        P("replica", "fsdp"),
        P("replica", "fsdp"),
        P("fsdp"),
        P("fsdp"),
    )
    return jax.shard_map(
        body,
        mesh=mesh,
        in_specs=placed,
        out_specs=(
            P("replica", "fsdp", None),
            P("replica", "fsdp", None),
            P("replica", "fsdp", None),
            P("fsdp"),
            P("fsdp"),
        ),
        check_vma=False,
    )
```
